512 devices in a mesh: wide: 64 (over y_lo, x, z), head: 8 (over y_hi, core).
Axes of the slice: x: 4, y: 8 (y_hi: 4, y_lo: 2; y = y_hi * 2 + y_lo), z: 8, core: 2. Of those that a mesh axis runs over, the one named last changes fastest.
Arguments:
- query: bfloat16 [4096, 16384], P('wide', 'head'), may hold values from -128 to 128
- key_new: bfloat16 [4096, 1024], P('wide', 'head'), may hold values from -7 to 7
- value_new: bfloat16 [4096, 1024], P('wide', 'head'), may hold values from -6 to 6
- key_cache: bfloat16 [1024, 128, 1024], P(('wide', 'head')), may hold values from -6 to 6
- value_cache: bfloat16 [1024, 128, 1024], P(('wide', 'head')), may hold values from -6 to 6
- page_table: int32 [64, 16], replicated, may hold values from 0 to 1023, as said below
- prefix_len: int32 [64], replicated, may hold values from 1 to 2048
Outputs:
- attended: bfloat16 [4096, 16384], P('wide', 'head')
The draws below stay inside these ranges and needn't reach their ends.
Inputs may be any that keep to these rules, and one draw needn't show every extreme that they name: `page_table`: slot s lies in store group s // 16 along wide; every slot holds exactly one page of one request. Each page of a request lies in its own store group: no store group holds more than one page of any one request.
All inputs are finite; a program needn't handle non-finite values.
Results may differ from the reference program's by a relative error of at most 0.015.
Values may be sent and summed in bfloat16 or wider, within the bound.
No kernel may reach another device: no remote copies, remote signals or barrier semaphores. Data moves between devices by JAX's collectives and lax.ppermute only.
A program may use at most 64 MiB of HBM per device.

```python
import jax
import jax.numpy as jnp
from jax import lax

QH = 128
KVH = 8
HD = 128
NEW = 64
MAXP = 16
PAGE = 128
CAP = 1
MAXLEN = 2048
REQUESTS = 64
TOKENS = 4096
SLOTS = 1024
N_WIDE = 64


def shared_rows(key):
    shared_base = jax.random.normal(jax.random.fold_in(key, 7), (TOKENS, KVH * HD), jnp.float32)
    shared_base = jnp.clip(shared_base, -6.0, 6.0)
    return shared_base


def draw_query(key, part):
    key = jax.random.fold_in(key, 303)
    drawn = jax.random.normal(jax.random.fold_in(key, 1), (TOKENS, QH * HD), jnp.float32)
    return jnp.clip(drawn, -6.0, 6.0).astype(jnp.bfloat16)


def draw_key_new(key, part):
    shared_base = shared_rows(key)
    return shared_base.astype(jnp.bfloat16)


def draw_page_table(key, part):
    key = jax.random.fold_in(key, 101)
    run_count = MAXP // CAP
    offsets = jax.random.permutation(jax.random.fold_in(key, 1), N_WIDE)[:run_count]
    rename = jax.random.permutation(jax.random.fold_in(key, 2), N_WIDE)
    start_order = jax.random.permutation(jax.random.fold_in(key, 3), N_WIDE)
    position = (start_order[:, None] + offsets[None, :]) % N_WIDE
    groups = rename[position]
    group_keys = jax.random.split(jax.random.fold_in(key, 4), N_WIDE)
    shuffles = jax.vmap(lambda single: jax.random.permutation(single, MAXP))(group_keys)
    page_index = jnp.arange(MAXP)
    run_index = page_index // CAP
    page_group = groups[:, run_index]
    slot_index = shuffles[page_group, page_index[None, :]]
    return (page_group * MAXP + slot_index).astype(jnp.int32)


def draw_prefix_len(key, part):
    key = jax.random.fold_in(key, 202)
    shrink = jax.random.randint(jax.random.fold_in(key, 1), (N_WIDE,), 0, 4)
    ceiling = jnp.right_shift(jnp.full((N_WIDE,), MAXLEN, jnp.int32), shrink)
    shortening = jax.random.randint(jax.random.fold_in(key, 2), (N_WIDE,), 0, 1024)
    length = ceiling - ceiling // 2 * shortening // 1024
    longest = jax.random.randint(jax.random.fold_in(key, 3), (), 0, N_WIDE)
    length = jnp.where(jnp.arange(N_WIDE) == longest, MAXLEN, length)
    return jnp.maximum(length, 1).astype(jnp.int32)


def level_of(stream_key, extent, shards, low, top_value):
    factor_of, own = 1.0, jax.random.fold_in(stream_key, 6)
    for axis_at, parts in shards:
        heights = jnp.exp(jax.random.uniform(jax.random.fold_in(own, axis_at), (parts,), jnp.float32, low / len(shards), top_value / len(shards)))
        factor_of = factor_of * jnp.repeat(heights, extent[axis_at] // parts).reshape([-1 if axis == axis_at else 1 for axis in range(len(extent))])
    return factor_of


def bell_draw(own_key, extent, width, reach, pieces=(), kind=jnp.bfloat16):
    array = width * jax.random.normal(own_key, extent, jnp.float32)
    if pieces:
        array = array * level_of(own_key, extent, pieces, -0.22, 0.18)
    return jnp.clip(array, -reach, reach).astype(kind)


def setup_inputs(seed: int = 0) -> dict:
    splits = jax.random.split(jax.random.key(seed), 8)
    return {
        "query": draw_query(jax.random.fold_in(splits[7], 71), 0),
        "key_new": draw_key_new(jax.random.fold_in(splits[7], 71), 0),
        "value_new": bell_draw(splits[2], (TOKENS, KVH * HD), 1.0, 6.0, ((0, 64), (1, 8))),
        "key_cache": bell_draw(splits[3], (SLOTS, PAGE, KVH * HD), 1.0, 6.0, ((0, 512),)),
        "value_cache": bell_draw(splits[4], (SLOTS, PAGE, KVH * HD), 1.0, 6.0, ((0, 512),)),
        "page_table": draw_page_table(jax.random.fold_in(splits[7], 71), 0),
        "prefix_len": draw_prefix_len(jax.random.fold_in(splits[7], 71), 0),
    }


def reference(query, key_new, value_new, key_cache, value_cache, page_table, prefix_len):
    group_size = QH // KVH
    queries = query.reshape(REQUESTS, NEW, KVH, group_size, HD)
    keys_new = key_new.reshape(REQUESTS, NEW, KVH, HD)
    values_new = value_new.reshape(REQUESTS, NEW, KVH, HD)
    causal = jnp.arange(NEW)[None, :] <= jnp.arange(NEW)[:, None]

    def attend(request_data):
        query_rows, fresh_k, fresh_v, page_ids, length = request_data
        old_k = jnp.take(key_cache, page_ids, axis=0).reshape(MAXLEN, KVH, HD)
        old_v = jnp.take(value_cache, page_ids, axis=0).reshape(MAXLEN, KVH, HD)
        all_keys = jnp.concatenate([old_k, fresh_k], axis=0).astype(jnp.float32)
        values = jnp.concatenate([old_v, fresh_v], axis=0).astype(jnp.float32)
        scores = jnp.einsum("tkge,ske->kgts", query_rows.astype(jnp.float32), all_keys) * (HD ** -0.5)
        prefix_seen = jnp.broadcast_to((jnp.arange(MAXLEN) < length)[None, :], (NEW, MAXLEN))
        visible = jnp.concatenate([prefix_seen, causal], axis=1)
        scores = jnp.where(visible, scores, -jnp.inf)
        highest = jnp.max(scores, axis=-1, keepdims=True)
        weights = jnp.exp(scores - highest)
        weight_sum = jnp.sum(weights, axis=-1)
        rounded = lax.optimization_barrier(weights.astype(jnp.bfloat16))
        probabilities = rounded.astype(jnp.float32)
        mixed = jnp.einsum("kgts,ske->tkge", probabilities, values)
        mixed = mixed / jnp.transpose(weight_sum, (2, 0, 1))[..., None]
        return mixed.astype(jnp.bfloat16).reshape(NEW, QH * HD)

    result = lax.map(attend, (queries, keys_new, values_new, page_table, prefix_len))
    return result.reshape(REQUESTS * NEW, QH * HD)
```

```python
import functools
import math

import jax
import jax.numpy as jnp
from jax import lax
from jax.experimental import pallas as pl
from jax.experimental.pallas import tpu as pltpu
from jax.sharding import Mesh, PartitionSpec as P

Y_LO, X, Z = 2, 4, 8
Y_HI, CORE = 4, 2
COLUMNS = Y_LO * X
HEADS = Y_HI * CORE
HD = 128
PAGE = 128
MAXP = 16
PIECE = PAGE // COLUMNS
PLANE = ("y_lo", "x", "y_hi", "core")
COLUMN = ("y_lo", "x")
SMALL_CAP = 16
FULL_CAP = 64
HIDDEN = -1e30
EXP2_SCALE = math.log2(math.e) / math.sqrt(HD)
PARAMS = pltpu.CompilerParams(vmem_limit_bytes=40 * 2**20)
VMEM = pl.BlockSpec(memory_space=pltpu.VMEM)
SMEM = pl.BlockSpec(memory_space=pltpu.SMEM)


def split_kernel(key_ref, value_ref, out_ref):
    for page in range(out_ref.shape[1]):
        for kind, source in enumerate((key_ref, value_ref)):
            for column in range(COLUMNS):
                rows = pl.ds(column * PIECE, PIECE)
                for head in range(HEADS):
                    out_ref[column * HEADS + head, page, kind] = source[
                        page, rows, head * HD : (head + 1) * HD
                    ]


def split_pages(key_cache, value_cache):
    stored = key_cache.shape[0]
    return pl.pallas_call(
        split_kernel,
        out_shape=jax.ShapeDtypeStruct((COLUMNS * HEADS, stored, 2, PIECE, HD), jnp.bfloat16),
        in_specs=[VMEM, VMEM],
        out_specs=VMEM,
        compiler_params=PARAMS,
        name="split_pages",
    )(key_cache, value_cache)


def to_plane_kernel(table_ref, held_ref, out_ref):
    cap = out_ref.shape[1]
    for plane in range(Z):

        @pl.loop(0, cap, unroll=8)
        def _(place):
            out_ref[plane, place] = held_ref[table_ref[plane, place]]


def pick_for_planes(table, held):
    return pl.pallas_call(
        to_plane_kernel,
        out_shape=jax.ShapeDtypeStruct(table.shape + held.shape[1:], jnp.bfloat16),
        in_specs=[SMEM, VMEM],
        out_specs=VMEM,
        compiler_params=PARAMS,
        name="pick_for_planes",
    )(table, held)


def to_request_kernel(table_ref, held_ref, out_ref):
    for column in range(COLUMNS):

        @pl.loop(0, MAXP, unroll=8)
        def _(page):
            place = table_ref[column, page]
            out_ref[column, 0, page] = held_ref[place, 0]
            out_ref[column, 1, page] = held_ref[place, 1]


def pick_for_requests(table, held):
    return pl.pallas_call(
        to_request_kernel,
        out_shape=jax.ShapeDtypeStruct((COLUMNS, 2, MAXP, PIECE, HD), jnp.bfloat16),
        in_specs=[SMEM, VMEM],
        out_specs=VMEM,
        compiler_params=PARAMS,
        name="pick_for_requests",
    )(table, held)


HEADS_PER_STEP = 4


def contract_last(left, right):
    return lax.dot_general(
        left, right, (((1,), (1,)), ((), ())), preferred_element_type=jnp.float32
    )


def attend_kernel(length_ref, query_ref, key_ref, value_ref, held_ref, out_ref):
    tokens = query_ref.shape[0]
    group = query_ref.shape[1] // HD
    rows = HEADS_PER_STEP * tokens
    keys = MAXP * PIECE
    length = length_ref[0]
    at = lax.broadcasted_iota(jnp.int32, (1, keys), 1)
    position = (at // PIECE) * PAGE + at % PIECE
    biases = [
        jnp.where(position + column * PIECE < length, 0.0, HIDDEN) for column in range(COLUMNS)
    ]
    token = lax.broadcasted_iota(jnp.int32, (rows, tokens), 0) % tokens
    causal = lax.broadcasted_iota(jnp.int32, (rows, tokens), 1) <= token
    for step in range(group // HEADS_PER_STEP):
        first = step * HEADS_PER_STEP
        query = jnp.concatenate(
            [
                query_ref[:, (first + n) * HD : (first + n + 1) * HD]
                for n in range(HEADS_PER_STEP)
            ],
            axis=0,
        )
        fresh = jnp.where(causal, contract_last(query, key_ref[...]), HIDDEN)
        scores = [
            contract_last(query, held_ref[column, 0].reshape(keys, HD)) + biases[column]
            for column in range(COLUMNS)
        ]
        top = functools.reduce(jnp.maximum, scores)
        highest = jnp.maximum(
            jnp.max(top, axis=1, keepdims=True), jnp.max(fresh, axis=1, keepdims=True)
        )
        fresh = jnp.exp2((fresh - highest) * EXP2_SCALE)
        mixed = jnp.dot(
            fresh.astype(jnp.bfloat16), value_ref[...], preferred_element_type=jnp.float32
        )
        total = None
        for column in range(COLUMNS):
            weights = jnp.exp2((scores[column] - highest) * EXP2_SCALE)
            total = weights if total is None else total + weights
            mixed += jnp.dot(
                weights.astype(jnp.bfloat16),
                held_ref[column, 1].reshape(keys, HD),
                preferred_element_type=jnp.float32,
            )
        weight_sum = jnp.sum(total, axis=1, keepdims=True) + jnp.sum(
            fresh, axis=1, keepdims=True
        )
        mixed = (mixed / weight_sum).astype(jnp.bfloat16)
        for n in range(HEADS_PER_STEP):
            out_ref[:, (first + n) * HD : (first + n + 1) * HD] = mixed[
                n * tokens : (n + 1) * tokens
            ]


def attend(length, query, key_new, value_new, held):
    return pl.pallas_call(
        attend_kernel,
        out_shape=jax.ShapeDtypeStruct(query.shape, jnp.bfloat16),
        in_specs=[SMEM, VMEM, VMEM, VMEM, VMEM],
        out_specs=VMEM,
        compiler_params=PARAMS,
        name="attend",
    )(length, query, key_new, value_new, held)


def exchange(array, axes):
    return lax.all_to_all(array, axes, split_axis=0, concat_axis=0, tiled=True)


def by_plane(array):
    array = array.reshape(COLUMNS, Z, MAXP)
    return jnp.swapaxes(array, 0, 1).reshape(Z, COLUMNS * MAXP)


def routes(page_table, prefix_len):
    live = jnp.arange(MAXP, dtype=jnp.int32)[None, :] * PAGE < prefix_len[:, None]
    pages, live = by_plane(page_table), by_plane(live)
    from_plane = jnp.where(live, pages // MAXP % Z, -1)
    in_plane = pages // (MAXP * Z) * MAXP + pages % MAXP
    count = pages.shape[1]
    order = jnp.arange(count, dtype=jnp.int32)
    same = from_plane[:, :, None] == from_plane[:, None, :]
    earlier = order[None, :] < order[:, None]
    place = jnp.sum((same & earlier[None]).astype(jnp.int32), axis=2)
    place = jnp.where(live, place, -1)
    return from_plane, in_plane, place


def tail(cap, query, key_new, value_new, pieces, from_plane, in_plane, place, length):
    own_plane = lax.axis_index("z")
    wanted = jnp.arange(cap, dtype=jnp.int32)
    chosen = (from_plane == own_plane)[:, None, :] & (place[:, None, :] == wanted[None, :, None])
    plane_table = jnp.sum(jnp.where(chosen, in_plane[:, None, :], 0), axis=2)
    own_from = lax.dynamic_index_in_dim(from_plane, own_plane, 0, keepdims=False)
    own_place = lax.dynamic_index_in_dim(place, own_plane, 0, keepdims=False)
    slots = (own_from * cap + own_place).reshape(COLUMNS, MAXP)
    request_table = jnp.where(own_place.reshape(COLUMNS, MAXP) >= 0, slots, slots[:, :1])
    sent = pick_for_planes(plane_table, pieces)
    gathered = exchange(sent, "z").reshape((Z * cap,) + pieces.shape[1:])
    ready = pick_for_requests(request_table, gathered)
    held = exchange(ready, COLUMN)
    return attend(length, query, key_new, value_new, held)


def body(query, key_new, value_new, key_cache, value_cache, page_table, prefix_len):
    own_request = lax.axis_index(("y_lo", "x", "z"))
    pieces = exchange(split_pages(key_cache, value_cache), PLANE)
    pieces = pieces.reshape((COLUMNS * MAXP,) + pieces.shape[2:])
    from_plane, in_plane, place = routes(page_table, prefix_len)
    length = lax.dynamic_slice_in_dim(prefix_len, own_request, 1)
    operands = (query, key_new, value_new, pieces, from_plane, in_plane, place, length)
    return lax.cond(
        jnp.max(place) < SMALL_CAP,
        functools.partial(tail, SMALL_CAP),
        functools.partial(tail, FULL_CAP),
        *operands,
    )


def solution(mesh):
    fine = Mesh(
        mesh.devices.reshape(Y_LO, X, Z, Y_HI, CORE), ("y_lo", "x", "z", "y_hi", "core")
    )
    wide, head = ("y_lo", "x", "z"), ("y_hi", "core")
    in_specs = (
        P(wide, head),
        P(wide, head),
        P(wide, head),
        P(wide + head, None, None),
        P(wide + head, None, None),
        P(),
        P(),
    )
    return jax.shard_map(
        body, mesh=fine, in_specs=in_specs, out_specs=P(wide, head), check_vma=False
    )
```

```python
import functools
import math

import jax
import jax.numpy as jnp
from jax import lax
from jax.experimental import pallas as pl
from jax.experimental.pallas import tpu as pltpu
from jax.sharding import Mesh, PartitionSpec as P

Y_LO, X, Z = 2, 4, 8
Y_HI, CORE = 4, 2
WIDE_AXES, HEAD_AXES = ("y_lo", "x", "z"), ("y_hi", "core")
WIDE = Y_LO * X * Z
HEADS = Y_HI * CORE
HD = 128
PAGE = 128
MAXP = 16
STORED = 2
PIECE = PAGE // WIDE
ROWS = STORED * 2 * PIECE
HIDDEN = -1e30
EXP2_SCALE = math.log2(math.e) / math.sqrt(HD)
PARAMS = pltpu.CompilerParams(vmem_limit_bytes=40 * 2**20)
VMEM = pl.BlockSpec(memory_space=pltpu.VMEM)
SMEM = pl.BlockSpec(memory_space=pltpu.SMEM)
HBM = pl.BlockSpec(memory_space=pltpu.HBM)

PARTS = 4
PART_TOKENS = PAGE // PARTS
PART_WIDE = WIDE // PARTS


def split_kernel(key_hbm, value_hbm, out_hbm, cache, ready, in_sems, out_sems):
    def fetch(part, kind):
        tokens = pl.ds(part * PART_TOKENS, PART_TOKENS)
        source = (key_hbm, value_hbm)[kind]
        return pltpu.make_async_copy(
            source.at[:, tokens], cache.at[kind, :, tokens], in_sems.at[part, kind]
        )

    def leave(part):
        rows = pl.ds(part * PART_WIDE, PART_WIDE)
        return pltpu.make_async_copy(ready.at[rows], out_hbm.at[rows], out_sems.at[part])

    for part in range(PARTS):
        for kind in range(2):
            fetch(part, kind).start()
    count = PART_WIDE * ROWS
    at = lax.broadcasted_iota(jnp.int32, (count, count), 0)
    source_row = (at % ROWS // PIECE) * PART_TOKENS + at // ROWS * PIECE + at % PIECE
    moved = source_row == lax.broadcasted_iota(jnp.int32, (count, count), 1)
    moved = jnp.where(moved, 1.0, 0.0).astype(jnp.bfloat16)
    for part in range(PARTS):
        for kind in range(2):
            fetch(part, kind).wait()
        tokens = slice(part * PART_TOKENS, (part + 1) * PART_TOKENS)
        rows = jnp.concatenate(
            [cache[kind, page, tokens] for page in range(STORED) for kind in range(2)], axis=0
        )
        rows = jnp.dot(moved, rows, preferred_element_type=jnp.float32)
        for pair in range(HEADS // 2):
            both = [
                rows[:, head * HD : (head + 1) * HD].reshape(PART_WIDE, ROWS, HD)
                for head in (2 * pair, 2 * pair + 1)
            ]
            ready[part * PART_WIDE : (part + 1) * PART_WIDE, pair] = jnp.concatenate(
                both, axis=1
            ).astype(jnp.bfloat16)
        leave(part).start()
    for part in range(PARTS):
        leave(part).wait()


def split_pages(key_cache, value_cache):
    shape = (WIDE, HEADS // 2, 2 * ROWS, HD)
    return pl.pallas_call(
        split_kernel,
        out_shape=jax.ShapeDtypeStruct(shape, jnp.bfloat16),
        in_specs=[HBM, HBM],
        out_specs=HBM,
        scratch_shapes=[
            pltpu.VMEM((2,) + key_cache.shape, jnp.bfloat16),
            pltpu.VMEM(shape, jnp.bfloat16),
            pltpu.SemaphoreType.DMA((PARTS, 2)),
            pltpu.SemaphoreType.DMA((PARTS,)),
        ],
        compiler_params=PARAMS,
        name="split_pages",
    )(key_cache, value_cache)


PICK_REQUESTS = 16


def pick_kernel(chosen_ref, held_ref, out_ref, spread):
    sources = held_ref.shape[0] * 2
    spread[...] = held_ref[...].reshape(sources * ROWS, HD).astype(jnp.float32)
    columns = []
    for quarter in range(2 * PIECE):
        column = [
            spread[pl.ds(page * 2 * PIECE + quarter, sources, stride=ROWS), :]
            for page in range(STORED)
        ]
        columns.append(jnp.concatenate(column, axis=0).astype(jnp.bfloat16))
    columns = jnp.concatenate(columns, axis=1)
    for step in range(WIDE // PICK_REQUESTS):
        first = step * PICK_REQUESTS
        picked = jnp.dot(
            chosen_ref[first * MAXP : (first + PICK_REQUESTS) * MAXP],
            columns,
            preferred_element_type=jnp.float32,
        ).astype(jnp.bfloat16)
        for request in range(PICK_REQUESTS):
            for quarter in range(2 * PIECE):
                out_ref[first + request, quarter * MAXP : (quarter + 1) * MAXP] = picked[
                    request * MAXP : (request + 1) * MAXP, quarter * HD : (quarter + 1) * HD
                ]


def pick_pages(chosen, held):
    shape = (WIDE, 2 * PIECE * MAXP, HD)
    return pl.pallas_call(
        pick_kernel,
        out_shape=jax.ShapeDtypeStruct(shape, jnp.bfloat16),
        in_specs=[VMEM, VMEM],
        out_specs=VMEM,
        scratch_shapes=[pltpu.VMEM((held.shape[0] * 2 * ROWS, HD), jnp.float32)],
        compiler_params=PARAMS,
        name="pick_pages",
    )(chosen, held)


HEADS_PER_STEP = 4
CHUNK_WIDE = 8


def contract_last(left, right):
    return lax.dot_general(
        left, right, (((1,), (1,)), ((), ())), preferred_element_type=jnp.float32
    )


def attend_kernel(length_ref, query_ref, key_ref, value_ref, held_ref, out_ref):
    tokens = query_ref.shape[0]
    group = query_ref.shape[1] // HD
    rows = HEADS_PER_STEP * tokens
    half = PIECE * MAXP
    keys = CHUNK_WIDE * half
    chunks = WIDE // CHUNK_WIDE
    length = length_ref[0]
    at = lax.broadcasted_iota(jnp.int32, (1, keys), 1)
    position = at % MAXP * PAGE + at // MAXP
    biases = [
        jnp.where(position + chunk * CHUNK_WIDE * PIECE < length, 0.0, HIDDEN)
        for chunk in range(chunks)
    ]
    token = lax.broadcasted_iota(jnp.int32, (rows, tokens), 0) % tokens
    causal = lax.broadcasted_iota(jnp.int32, (rows, tokens), 1) <= token

    def held(chunk, kind):
        block = held_ref[
            chunk * CHUNK_WIDE : (chunk + 1) * CHUNK_WIDE, kind * half : (kind + 1) * half
        ]
        return block.reshape(keys, HD)

    for step in range(group // HEADS_PER_STEP):
        first = step * HEADS_PER_STEP
        query = jnp.concatenate(
            [
                query_ref[:, (first + n) * HD : (first + n + 1) * HD]
                for n in range(HEADS_PER_STEP)
            ],
            axis=0,
        )
        fresh = jnp.where(causal, contract_last(query, key_ref[...]), HIDDEN)
        scores = [
            contract_last(query, held(chunk, 0)) + biases[chunk] for chunk in range(chunks)
        ]
        top = functools.reduce(jnp.maximum, scores)
        highest = jnp.maximum(
            jnp.max(top, axis=1, keepdims=True), jnp.max(fresh, axis=1, keepdims=True)
        )
        fresh = jnp.exp2((fresh - highest) * EXP2_SCALE)
        mixed = jnp.dot(
            fresh.astype(jnp.bfloat16), value_ref[...], preferred_element_type=jnp.float32
        )
        total = None
        for chunk in range(chunks):
            weights = jnp.exp2((scores[chunk] - highest) * EXP2_SCALE)
            total = weights if total is None else total + weights
            mixed += jnp.dot(
                weights.astype(jnp.bfloat16), held(chunk, 1), preferred_element_type=jnp.float32
            )
        weight_sum = jnp.sum(total, axis=1, keepdims=True) + jnp.sum(
            fresh, axis=1, keepdims=True
        )
        mixed = (mixed / weight_sum).astype(jnp.bfloat16)
        for n in range(HEADS_PER_STEP):
            out_ref[:, (first + n) * HD : (first + n + 1) * HD] = mixed[
                n * tokens : (n + 1) * tokens
            ]


def attend(length, query, key_new, value_new, held):
    return pl.pallas_call(
        attend_kernel,
        out_shape=jax.ShapeDtypeStruct(query.shape, jnp.bfloat16),
        in_specs=[SMEM, VMEM, VMEM, VMEM, VMEM],
        out_specs=VMEM,
        compiler_params=PARAMS,
        name="attend",
    )(length, query, key_new, value_new, held)


def exchange(array, axes):
    return lax.all_to_all(array, axes, split_axis=0, concat_axis=0, tiled=True)


def body(query, key_new, value_new, key_cache, value_cache, page_table, prefix_len):
    own_request = lax.axis_index(WIDE_AXES)
    length = lax.dynamic_slice_in_dim(prefix_len, own_request, 1)
    sources = WIDE * HEADS
    pages = page_table.reshape(-1)
    column = pages % STORED * sources + pages // STORED
    every = jnp.arange(STORED * sources, dtype=jnp.int32)
    chosen = (column[:, None] == every[None, :]).astype(jnp.bfloat16)
    pieces = split_pages(key_cache, value_cache).reshape(sources, ROWS, HD)
    pieces = exchange(pieces, WIDE_AXES + HEAD_AXES)
    picked = pick_pages(chosen, pieces.reshape(sources // 2, 2 * ROWS, HD))
    held = exchange(picked, WIDE_AXES)
    return attend(length, query, key_new, value_new, held)


def solution(mesh):
    fine = Mesh(mesh.devices.reshape(Y_LO, X, Z, Y_HI, CORE), WIDE_AXES + HEAD_AXES)
    in_specs = (
        P(WIDE_AXES, HEAD_AXES),
        P(WIDE_AXES, HEAD_AXES),
        P(WIDE_AXES, HEAD_AXES),
        P(WIDE_AXES + HEAD_AXES, None, None),
        P(WIDE_AXES + HEAD_AXES, None, None),
        P(),
        P(),
    )
    return jax.shard_map(
        body,
        mesh=fine,
        in_specs=in_specs,
        out_specs=P(WIDE_AXES, HEAD_AXES),
        check_vma=False,
    )
```

```python
import functools
import math

import jax
import jax.numpy as jnp
from jax import lax
from jax.experimental import pallas as pl
from jax.experimental.pallas import tpu as pltpu
from jax.sharding import Mesh, PartitionSpec as P

Y_LO, X, Z = 2, 4, 8
Y_HI, CORE = 4, 2
WIDE_AXES, HEAD_AXES = ("y_lo", "x", "z"), ("y_hi", "core")
WIDE = Y_LO * X * Z
HEADS = Y_HI * CORE
HD = 128
PAGE = 128
MAXP = 16
STORED = 2
PIECE = PAGE // WIDE
ROWS = STORED * 2 * PIECE
HIDDEN = -1e30
EXP2_SCALE = math.log2(math.e) / math.sqrt(HD)
PARAMS = pltpu.CompilerParams(vmem_limit_bytes=40 * 2**20)
ALL_PARAMS = pltpu.CompilerParams(vmem_limit_bytes=63 * 2**20)
VMEM = pl.BlockSpec(memory_space=pltpu.VMEM)
HBM = pl.BlockSpec(memory_space=pltpu.HBM)

PARTS = 2
PART_TOKENS = PAGE // PARTS
PART_WIDE = WIDE // PARTS


def split_kernel(key_hbm, value_hbm, out_hbm, cache, ready, in_sems, out_sems):
    def fetch(part, kind):
        tokens = pl.ds(part * PART_TOKENS, PART_TOKENS)
        source = (key_hbm, value_hbm)[kind]
        return pltpu.make_async_copy(
            source.at[:, tokens], cache.at[kind, :, tokens], in_sems.at[part, kind]
        )

    def leave(part):
        rows = pl.ds(part * PART_WIDE, PART_WIDE)
        return pltpu.make_async_copy(ready.at[rows], out_hbm.at[rows], out_sems.at[part])

    for part in range(PARTS):
        for kind in range(2):
            fetch(part, kind).start()
    count = PART_WIDE * ROWS
    at = lax.broadcasted_iota(jnp.int32, (count, count), 0)
    source_row = (at % ROWS // PIECE) * PART_TOKENS + at // ROWS * PIECE + at % PIECE
    moved = source_row == lax.broadcasted_iota(jnp.int32, (count, count), 1)
    moved = jnp.where(moved, 1.0, 0.0).astype(jnp.bfloat16)
    for part in range(PARTS):
        for kind in range(2):
            fetch(part, kind).wait()
        tokens = slice(part * PART_TOKENS, (part + 1) * PART_TOKENS)
        rows = jnp.concatenate(
            [cache[kind, page, tokens] for page in range(STORED) for kind in range(2)], axis=0
        )
        rows = jnp.dot(moved, rows, preferred_element_type=jnp.float32)
        for pair in range(HEADS // 2):
            both = [
                rows[:, head * HD : (head + 1) * HD].reshape(PART_WIDE, ROWS, HD)
                for head in (2 * pair, 2 * pair + 1)
            ]
            ready[part * PART_WIDE : (part + 1) * PART_WIDE, pair] = jnp.concatenate(
                both, axis=1
            ).astype(jnp.bfloat16)
        leave(part).start()
    for part in range(PARTS):
        leave(part).wait()


def split_pages(key_cache, value_cache):
    shape = (WIDE, HEADS // 2, 2 * ROWS, HD)
    return pl.pallas_call(
        split_kernel,
        out_shape=jax.ShapeDtypeStruct(shape, jnp.bfloat16),
        in_specs=[HBM, HBM],
        out_specs=HBM,
        scratch_shapes=[
            pltpu.VMEM((2,) + key_cache.shape, jnp.bfloat16),
            pltpu.VMEM(shape, jnp.bfloat16),
            pltpu.SemaphoreType.DMA((PARTS, 2)),
            pltpu.SemaphoreType.DMA((PARTS,)),
        ],
        compiler_params=ALL_PARAMS,
        name="split_pages",
    )(key_cache, value_cache)


PICK_REQUESTS = 32
PICK_STEPS = WIDE // PICK_REQUESTS


def pick_kernel(chosen_ref, held_ref, out_hbm, spread, ready, sems):
    sources = held_ref.shape[0] * 2

    def leave(step):
        requests = pl.ds(step * PICK_REQUESTS, PICK_REQUESTS)
        return pltpu.make_async_copy(ready.at[requests], out_hbm.at[requests], sems.at[step])

    spread[...] = held_ref[...].reshape(sources * ROWS, HD).astype(jnp.float32)
    columns = []
    for quarter in range(2 * PIECE):
        column = [
            spread[pl.ds(page * 2 * PIECE + quarter, sources, stride=ROWS), :]
            for page in range(STORED)
        ]
        columns.append(jnp.concatenate(column, axis=0).astype(jnp.bfloat16))
    columns = jnp.concatenate(columns, axis=1)
    for step in range(PICK_STEPS):
        first = step * PICK_REQUESTS
        picked = jnp.dot(
            chosen_ref[first * MAXP : (first + PICK_REQUESTS) * MAXP],
            columns,
            preferred_element_type=jnp.float32,
        ).astype(jnp.bfloat16)
        for request in range(PICK_REQUESTS):
            for quarter in range(2 * PIECE):
                ready[first + request, quarter * MAXP : (quarter + 1) * MAXP] = picked[
                    request * MAXP : (request + 1) * MAXP, quarter * HD : (quarter + 1) * HD
                ]
        leave(step).start()
    for step in range(PICK_STEPS):
        leave(step).wait()


def pick_pages(chosen, held):
    shape = (WIDE, 2 * PIECE * MAXP, HD)
    return pl.pallas_call(
        pick_kernel,
        out_shape=jax.ShapeDtypeStruct(shape, jnp.bfloat16),
        in_specs=[VMEM, VMEM],
        out_specs=HBM,
        scratch_shapes=[
            pltpu.VMEM((held.shape[0] * 2 * ROWS, HD), jnp.float32),
            pltpu.VMEM(shape, jnp.bfloat16),
            pltpu.SemaphoreType.DMA((PICK_STEPS,)),
        ],
        compiler_params=PARAMS,
        name="pick_pages",
    )(chosen, held)


HEADS_PER_STEP = 8
CHUNK_WIDE = 8


def contract_last(left, right):
    return lax.dot_general(
        left, right, (((1,), (1,)), ((), ())), preferred_element_type=jnp.float32
    )


def attend_kernel(
    query_ref, key_ref, value_ref, held_ref, seen_ref, out_hbm, keys_ref, values_ref, mixed_ref, sems
):
    tokens = key_ref.shape[0]
    group = query_ref.shape[1] // HD
    rows = HEADS_PER_STEP * tokens
    width = HEADS_PER_STEP * HD
    half = PIECE * MAXP
    count = CHUNK_WIDE * half
    chunks = WIDE // CHUNK_WIDE
    steps = group // HEADS_PER_STEP

    def leave(step):
        columns = pl.ds(step * width, width)
        return pltpu.make_async_copy(mixed_ref.at[step], out_hbm.at[:, columns], sems.at[step])

    first_key = held_ref[0, 0:1, :]
    for chunk in range(chunks):
        wide = slice(chunk * CHUNK_WIDE, (chunk + 1) * CHUNK_WIDE)
        at = slice(chunk * count, (chunk + 1) * count)
        seen = seen_ref[at]
        visible = seen > 0
        keys_ref[at] = jnp.where(visible, held_ref[wide, :half].reshape(count, HD), first_key)
        values = held_ref[wide, half:].reshape(count, HD)
        values_ref[at, :HD] = jnp.where(visible, values, jnp.zeros_like(values))
        values_ref[at, HD:] = seen
    fresh_values = jnp.concatenate(
        [value_ref[...], jnp.ones((tokens, HD), jnp.bfloat16)], axis=1
    )
    token = lax.broadcasted_iota(jnp.int32, (rows, tokens), 0) % tokens
    causal = lax.broadcasted_iota(jnp.int32, (rows, tokens), 1) <= token
    for step in range(steps):
        query = jnp.concatenate(
            [
                query_ref[:, head * HD : (head + 1) * HD]
                for head in range(step * HEADS_PER_STEP, (step + 1) * HEADS_PER_STEP)
            ],
            axis=0,
        )
        fresh = jnp.where(causal, contract_last(query, key_ref[...]), HIDDEN)
        scores = [
            contract_last(query, keys_ref[chunk * count : (chunk + 1) * count])
            for chunk in range(chunks)
        ]
        top = functools.reduce(jnp.maximum, scores)
        highest = jnp.maximum(
            jnp.max(top, axis=1, keepdims=True), jnp.max(fresh, axis=1, keepdims=True)
        )
        mixed = jnp.dot(
            jnp.exp2((fresh - highest) * EXP2_SCALE).astype(jnp.bfloat16),
            fresh_values,
            preferred_element_type=jnp.float32,
        )
        weights = [jnp.exp2((part - highest) * EXP2_SCALE).astype(jnp.bfloat16) for part in scores]
        mixed += jnp.dot(
            jnp.concatenate(weights, axis=1), values_ref[...], preferred_element_type=jnp.float32
        )
        mixed = (mixed[:, :HD] / mixed[:, HD:]).astype(jnp.bfloat16)
        for n in range(HEADS_PER_STEP):
            mixed_ref[step, :, n * HD : (n + 1) * HD] = mixed[n * tokens : (n + 1) * tokens]
        leave(step).start()
    for step in range(steps):
        leave(step).wait()


def attend(query, key_new, value_new, held, seen):
    tokens, width = query.shape
    keys = WIDE * PIECE * MAXP
    steps = width // HD // HEADS_PER_STEP
    return pl.pallas_call(
        attend_kernel,
        out_shape=jax.ShapeDtypeStruct((tokens, width), jnp.bfloat16),
        in_specs=[VMEM] * 5,
        out_specs=HBM,
        scratch_shapes=[
            pltpu.VMEM((keys, HD), jnp.bfloat16),
            pltpu.VMEM((keys, 2 * HD), jnp.bfloat16),
            pltpu.VMEM((steps, tokens, HEADS_PER_STEP * HD), jnp.bfloat16),
            pltpu.SemaphoreType.DMA((steps,)),
        ],
        compiler_params=PARAMS,
        name="attend",
    )(query, key_new, value_new, held, seen)


def exchange(array, axes):
    return lax.all_to_all(array, axes, split_axis=0, concat_axis=0, tiled=True)


def body(query, key_new, value_new, key_cache, value_cache, page_table, prefix_len):
    own_request = lax.axis_index(WIDE_AXES)
    length = jnp.take(prefix_len, own_request)
    at = jnp.arange(WIDE * PIECE * MAXP, dtype=jnp.int32)
    seen = at % MAXP * PAGE + at // MAXP < length
    seen = jnp.broadcast_to(seen[:, None], (at.shape[0], HD)).astype(jnp.bfloat16)
    sources = WIDE * HEADS
    pages = page_table.reshape(-1)
    column = pages % STORED * sources + pages // STORED
    every = jnp.arange(STORED * sources, dtype=jnp.int32)
    chosen = (column[:, None] == every[None, :]).astype(jnp.bfloat16)
    pieces = split_pages(key_cache, value_cache).reshape(sources, ROWS, HD)
    pieces = exchange(pieces, WIDE_AXES + HEAD_AXES)
    picked = pick_pages(chosen, pieces.reshape(sources // 2, 2 * ROWS, HD))
    held = exchange(picked, WIDE_AXES)
    return attend(query, key_new, value_new, held, seen)


def solution(mesh):
    fine = Mesh(mesh.devices.reshape(Y_LO, X, Z, Y_HI, CORE), WIDE_AXES + HEAD_AXES)
    in_specs = (
        P(WIDE_AXES, HEAD_AXES),
        P(WIDE_AXES, HEAD_AXES),
        P(WIDE_AXES, HEAD_AXES),
        P(WIDE_AXES + HEAD_AXES, None, None),
        P(WIDE_AXES + HEAD_AXES, None, None),
        P(),
        P(),
    )
    return jax.shard_map(
        body,
        mesh=fine,
        in_specs=in_specs,
        out_specs=P(WIDE_AXES, HEAD_AXES),
        check_vma=False,
    )
```

```python
import functools
import math

import jax
import jax.numpy as jnp
from jax import lax
from jax.experimental import pallas as pl
from jax.experimental.pallas import tpu as pltpu
from jax.sharding import Mesh, PartitionSpec as P

Y_LO, X, Z = 2, 4, 8
Y_HI, CORE = 4, 2
WIDE_AXES, HEAD_AXES = ("y_lo", "x", "z"), ("y_hi", "core")
WIDE = Y_LO * X * Z
HEADS = Y_HI * CORE
HD = 128
PAGE = 128
MAXP = 16
STORED = 2
PIECE = PAGE // WIDE
ROWS = STORED * 2 * PIECE
HIDDEN = -1e30
EXP2_SCALE = math.log2(math.e) / math.sqrt(HD)
PARAMS = pltpu.CompilerParams(vmem_limit_bytes=40 * 2**20)
ALL_PARAMS = pltpu.CompilerParams(vmem_limit_bytes=63 * 2**20)
VMEM = pl.BlockSpec(memory_space=pltpu.VMEM)
HBM = pl.BlockSpec(memory_space=pltpu.HBM)
ANY = pl.BlockSpec(memory_space=pl.ANY)

PARTS = 2
PART_TOKENS = PAGE // PARTS
PART_WIDE = WIDE // PARTS


def split_kernel(key_hbm, value_hbm, out_hbm, cache, ready, in_sems, out_sems):
    def fetch(part, kind):
        tokens = pl.ds(part * PART_TOKENS, PART_TOKENS)
        source = (key_hbm, value_hbm)[kind]
        return pltpu.make_async_copy(
            source.at[:, tokens], cache.at[kind, :, tokens], in_sems.at[part, kind]
        )

    def leave(part):
        rows = pl.ds(part * PART_WIDE, PART_WIDE)
        return pltpu.make_async_copy(ready.at[rows], out_hbm.at[rows], out_sems.at[part])

    for part in range(PARTS):
        for kind in range(2):
            fetch(part, kind).start()
    count = PART_WIDE * ROWS
    at = lax.broadcasted_iota(jnp.int32, (count, count), 0)
    source_row = (at % ROWS // PIECE) * PART_TOKENS + at // ROWS * PIECE + at % PIECE
    moved = source_row == lax.broadcasted_iota(jnp.int32, (count, count), 1)
    moved = jnp.where(moved, 1.0, 0.0).astype(jnp.bfloat16)
    for part in range(PARTS):
        for kind in range(2):
            fetch(part, kind).wait()
        tokens = slice(part * PART_TOKENS, (part + 1) * PART_TOKENS)
        rows = jnp.concatenate(
            [cache[kind, page, tokens] for page in range(STORED) for kind in range(2)], axis=0
        )
        rows = jnp.dot(moved, rows, preferred_element_type=jnp.float32)
        for pair in range(HEADS // 2):
            both = [
                rows[:, head * HD : (head + 1) * HD].reshape(PART_WIDE, ROWS, HD)
                for head in (2 * pair, 2 * pair + 1)
            ]
            ready[part * PART_WIDE : (part + 1) * PART_WIDE, pair] = jnp.concatenate(
                both, axis=1
            ).astype(jnp.bfloat16)
        leave(part).start()
    for part in range(PARTS):
        leave(part).wait()


def split_pages(key_cache, value_cache):
    shape = (WIDE, HEADS // 2, 2 * ROWS, HD)
    return pl.pallas_call(
        split_kernel,
        out_shape=jax.ShapeDtypeStruct(shape, jnp.bfloat16),
        in_specs=[HBM, HBM],
        out_specs=HBM,
        scratch_shapes=[
            pltpu.VMEM((2,) + key_cache.shape, jnp.bfloat16),
            pltpu.VMEM(shape, jnp.bfloat16),
            pltpu.SemaphoreType.DMA((PARTS, 2)),
            pltpu.SemaphoreType.DMA((PARTS,)),
        ],
        compiler_params=ALL_PARAMS,
        name="split_pages",
    )(key_cache, value_cache)


PICK_REQUESTS = 32
PICK_STEPS = WIDE // PICK_REQUESTS


def pick_kernel(chosen_ref, held_ref, seen_any, out_hbm, spread, ready, sems):
    del seen_any
    sources = held_ref.shape[0] * 2

    def leave(step):
        requests = pl.ds(step * PICK_REQUESTS, PICK_REQUESTS)
        return pltpu.make_async_copy(ready.at[requests], out_hbm.at[requests], sems.at[step])

    spread[...] = held_ref[...].reshape(sources * ROWS, HD).astype(jnp.float32)
    columns = []
    for quarter in range(2 * PIECE):
        column = [
            spread[pl.ds(page * 2 * PIECE + quarter, sources, stride=ROWS), :]
            for page in range(STORED)
        ]
        columns.append(jnp.concatenate(column, axis=0).astype(jnp.bfloat16))
    columns = jnp.concatenate(columns, axis=1)
    for step in range(PICK_STEPS):
        first = step * PICK_REQUESTS
        picked = jnp.dot(
            chosen_ref[first * MAXP : (first + PICK_REQUESTS) * MAXP],
            columns,
            preferred_element_type=jnp.float32,
        ).astype(jnp.bfloat16)
        for request in range(PICK_REQUESTS):
            for quarter in range(2 * PIECE):
                ready[first + request, quarter * MAXP : (quarter + 1) * MAXP] = picked[
                    request * MAXP : (request + 1) * MAXP, quarter * HD : (quarter + 1) * HD
                ]
        leave(step).start()
    for step in range(PICK_STEPS):
        leave(step).wait()


def pick_pages(chosen, held, seen):
    shape = (WIDE, 2 * PIECE * MAXP, HD)
    return pl.pallas_call(
        pick_kernel,
        out_shape=jax.ShapeDtypeStruct(shape, jnp.bfloat16),
        in_specs=[VMEM, VMEM, ANY],
        out_specs=HBM,
        scratch_shapes=[
            pltpu.VMEM((held.shape[0] * 2 * ROWS, HD), jnp.float32),
            pltpu.VMEM(shape, jnp.bfloat16),
            pltpu.SemaphoreType.DMA((PICK_STEPS,)),
        ],
        compiler_params=PARAMS,
        name="pick_pages",
    )(chosen, held, seen)


HEADS_PER_STEP = 8
CHUNK_WIDE = 8


def contract_last(left, right):
    return lax.dot_general(
        left, right, (((1,), (1,)), ((), ())), preferred_element_type=jnp.float32
    )


def attend_kernel(
    query_ref, key_ref, value_ref, held_ref, seen_ref, out_hbm, keys_ref, values_ref, mixed_ref, sems
):
    tokens = key_ref.shape[0]
    group = query_ref.shape[1] // HD
    rows = HEADS_PER_STEP * tokens
    width = HEADS_PER_STEP * HD
    half = PIECE * MAXP
    count = CHUNK_WIDE * half
    chunks = WIDE // CHUNK_WIDE
    steps = group // HEADS_PER_STEP

    def leave(step):
        columns = pl.ds(step * width, width)
        return pltpu.make_async_copy(mixed_ref.at[step], out_hbm.at[:, columns], sems.at[step])

    first_key = held_ref[0, 0:1, :]
    for chunk in range(chunks):
        wide = slice(chunk * CHUNK_WIDE, (chunk + 1) * CHUNK_WIDE)
        at = slice(chunk * count, (chunk + 1) * count)
        seen = seen_ref[at]
        visible = seen > 0
        keys_ref[at] = jnp.where(visible, held_ref[wide, :half].reshape(count, HD), first_key)
        values = held_ref[wide, half:].reshape(count, HD)
        values_ref[at, :HD] = jnp.where(visible, values, jnp.zeros_like(values))
        values_ref[at, HD:] = seen
    fresh_values = jnp.concatenate(
        [value_ref[...], jnp.ones((tokens, HD), jnp.bfloat16)], axis=1
    )
    token = lax.broadcasted_iota(jnp.int32, (rows, tokens), 0) % tokens
    causal = lax.broadcasted_iota(jnp.int32, (rows, tokens), 1) <= token
    for step in range(steps):
        query = jnp.concatenate(
            [
                query_ref[:, head * HD : (head + 1) * HD]
                for head in range(step * HEADS_PER_STEP, (step + 1) * HEADS_PER_STEP)
            ],
            axis=0,
        )
        fresh = jnp.where(causal, contract_last(query, key_ref[...]), HIDDEN)
        scores = [
            contract_last(query, keys_ref[chunk * count : (chunk + 1) * count])
            for chunk in range(chunks)
        ]
        top = functools.reduce(jnp.maximum, scores)
        highest = jnp.maximum(
            jnp.max(top, axis=1, keepdims=True), jnp.max(fresh, axis=1, keepdims=True)
        )
        mixed = jnp.dot(
            jnp.exp2((fresh - highest) * EXP2_SCALE).astype(jnp.bfloat16),
            fresh_values,
            preferred_element_type=jnp.float32,
        )
        weights = [jnp.exp2((part - highest) * EXP2_SCALE).astype(jnp.bfloat16) for part in scores]
        mixed += jnp.dot(
            jnp.concatenate(weights, axis=1), values_ref[...], preferred_element_type=jnp.float32
        )
        mixed = (mixed[:, :HD] / mixed[:, HD:]).astype(jnp.bfloat16)
        for n in range(HEADS_PER_STEP):
            mixed_ref[step, :, n * HD : (n + 1) * HD] = mixed[n * tokens : (n + 1) * tokens]
        leave(step).start()
    for step in range(steps):
        leave(step).wait()


def attend(query, key_new, value_new, held, seen):
    tokens, width = query.shape
    keys = WIDE * PIECE * MAXP
    steps = width // HD // HEADS_PER_STEP
    return pl.pallas_call(
        attend_kernel,
        out_shape=jax.ShapeDtypeStruct((tokens, width), jnp.bfloat16),
        in_specs=[VMEM] * 5,
        out_specs=HBM,
        scratch_shapes=[
            pltpu.VMEM((keys, HD), jnp.bfloat16),
            pltpu.VMEM((keys, 2 * HD), jnp.bfloat16),
            pltpu.VMEM((steps, tokens, HEADS_PER_STEP * HD), jnp.bfloat16),
            pltpu.SemaphoreType.DMA((steps,)),
        ],
        compiler_params=PARAMS,
        name="attend",
    )(query, key_new, value_new, held, seen)


def exchange(array, axes):
    return lax.all_to_all(array, axes, split_axis=0, concat_axis=0, tiled=True)


def body(query, key_new, value_new, key_cache, value_cache, page_table, prefix_len):
    own_request = lax.axis_index(WIDE_AXES)
    length = jnp.take(prefix_len, own_request)
    at = jnp.arange(WIDE * PIECE * MAXP, dtype=jnp.int32)
    seen = at % MAXP * PAGE + at // MAXP < length
    seen = jnp.broadcast_to(seen[:, None], (at.shape[0], HD)).astype(jnp.bfloat16)
    sources = WIDE * HEADS
    pages = page_table.reshape(-1)
    column = pages % STORED * sources + pages // STORED
    every = jnp.arange(STORED * sources, dtype=jnp.int32)
    chosen = (column[:, None] == every[None, :]).astype(jnp.bfloat16)
    pieces = split_pages(key_cache, value_cache).reshape(sources, ROWS, HD)
    pieces = exchange(pieces, WIDE_AXES + HEAD_AXES)
    picked = pick_pages(chosen, pieces.reshape(sources // 2, 2 * ROWS, HD), seen)
    held = exchange(picked, WIDE_AXES)
    return attend(query, key_new, value_new, held, seen)


def solution(mesh):
    fine = Mesh(mesh.devices.reshape(Y_LO, X, Z, Y_HI, CORE), WIDE_AXES + HEAD_AXES)
    in_specs = (
        P(WIDE_AXES, HEAD_AXES),
        P(WIDE_AXES, HEAD_AXES),
        P(WIDE_AXES, HEAD_AXES),
        P(WIDE_AXES + HEAD_AXES, None, None),
        P(WIDE_AXES + HEAD_AXES, None, None),
        P(),
        P(),
    )
    return jax.shard_map(
        body,
        mesh=fine,
        in_specs=in_specs,
        out_specs=P(WIDE_AXES, HEAD_AXES),
        check_vma=False,
    )
```

```python
import functools
import math

import jax
import jax.numpy as jnp
from jax import lax
from jax.experimental import pallas as pl
from jax.experimental.pallas import tpu as pltpu
from jax.sharding import Mesh, PartitionSpec as P

Y_LO, X, Z = 2, 4, 8
Y_HI, CORE = 4, 2
WIDE_AXES, HEAD_AXES = ("y_lo", "x", "z"), ("y_hi", "core")
WIDE = Y_LO * X * Z
HEADS = Y_HI * CORE
HD = 128
PAGE = 128
MAXP = 16
STORED = 2
PIECE = PAGE // WIDE
ROWS = STORED * 2 * PIECE
HIDDEN = -1e30
EXP2_SCALE = math.log2(math.e) / math.sqrt(HD)
PARAMS = pltpu.CompilerParams(vmem_limit_bytes=40 * 2**20)
ALL_PARAMS = pltpu.CompilerParams(vmem_limit_bytes=63 * 2**20)
VMEM = pl.BlockSpec(memory_space=pltpu.VMEM)
HBM = pl.BlockSpec(memory_space=pltpu.HBM)
ANY = pl.BlockSpec(memory_space=pl.ANY)

PARTS = 2
PART_TOKENS = PAGE // PARTS
PART_WIDE = WIDE // PARTS


def split_kernel(key_hbm, value_hbm, out_hbm, cache, ready, in_sems, out_sems):
    def fetch(part, kind):
        tokens = pl.ds(part * PART_TOKENS, PART_TOKENS)
        source = (key_hbm, value_hbm)[kind]
        return pltpu.make_async_copy(
            source.at[:, tokens], cache.at[kind, :, tokens], in_sems.at[part, kind]
        )

    def leave(part):
        rows = pl.ds(part * PART_WIDE, PART_WIDE)
        return pltpu.make_async_copy(ready.at[rows], out_hbm.at[rows], out_sems.at[part])

    for part in range(PARTS):
        for kind in range(2):
            fetch(part, kind).start()
    count = PART_WIDE * ROWS
    at = lax.broadcasted_iota(jnp.int32, (count, count), 0)
    source_row = (at % ROWS // PIECE) * PART_TOKENS + at // ROWS * PIECE + at % PIECE
    moved = source_row == lax.broadcasted_iota(jnp.int32, (count, count), 1)
    moved = jnp.where(moved, 1.0, 0.0).astype(jnp.bfloat16)
    for part in range(PARTS):
        for kind in range(2):
            fetch(part, kind).wait()
        tokens = slice(part * PART_TOKENS, (part + 1) * PART_TOKENS)
        rows = jnp.concatenate(
            [cache[kind, page, tokens] for page in range(STORED) for kind in range(2)], axis=0
        )
        rows = jnp.dot(moved, rows, preferred_element_type=jnp.float32)
        for pair in range(HEADS // 2):
            both = [
                rows[:, head * HD : (head + 1) * HD].reshape(PART_WIDE, ROWS, HD)
                for head in (2 * pair, 2 * pair + 1)
            ]
            ready[part * PART_WIDE : (part + 1) * PART_WIDE, pair] = jnp.concatenate(
                both, axis=1
            ).astype(jnp.bfloat16)
        leave(part).start()
    for part in range(PARTS):
        leave(part).wait()


def split_pages(key_cache, value_cache):
    shape = (WIDE, HEADS // 2, 2 * ROWS, HD)
    return pl.pallas_call(
        split_kernel,
        out_shape=jax.ShapeDtypeStruct(shape, jnp.bfloat16),
        in_specs=[HBM, HBM],
        out_specs=HBM,
        scratch_shapes=[
            pltpu.VMEM((2,) + key_cache.shape, jnp.bfloat16),
            pltpu.VMEM(shape, jnp.bfloat16),
            pltpu.SemaphoreType.DMA((PARTS, 2)),
            pltpu.SemaphoreType.DMA((PARTS,)),
        ],
        compiler_params=ALL_PARAMS,
        name="split_pages",
    )(key_cache, value_cache)


PICK_REQUESTS = 32
PICK_STEPS = WIDE // PICK_REQUESTS


def pick_kernel(chosen_ref, held_ref, seen_any, out_hbm, spread, ready, sems):
    del seen_any
    sources = held_ref.shape[0] * 2

    def leave(step):
        requests = pl.ds(step * PICK_REQUESTS, PICK_REQUESTS)
        return pltpu.make_async_copy(ready.at[requests], out_hbm.at[requests], sems.at[step])

    spread[...] = held_ref[...].reshape(sources * ROWS, HD).astype(jnp.float32)
    columns = []
    for quarter in range(2 * PIECE):
        column = [
            spread[pl.ds(page * 2 * PIECE + quarter, sources, stride=ROWS), :]
            for page in range(STORED)
        ]
        columns.append(jnp.concatenate(column, axis=0).astype(jnp.bfloat16))
    columns = jnp.concatenate(columns, axis=1)
    for step in range(PICK_STEPS):
        first = step * PICK_REQUESTS
        picked = jnp.dot(
            chosen_ref[first * MAXP : (first + PICK_REQUESTS) * MAXP],
            columns,
            preferred_element_type=jnp.float32,
        ).astype(jnp.bfloat16)
        for request in range(PICK_REQUESTS):
            for quarter in range(2 * PIECE):
                ready[first + request, quarter * MAXP : (quarter + 1) * MAXP] = picked[
                    request * MAXP : (request + 1) * MAXP, quarter * HD : (quarter + 1) * HD
                ]
        leave(step).start()
    for step in range(PICK_STEPS):
        leave(step).wait()


def pick_pages(chosen, held, seen):
    shape = (WIDE, 2 * PIECE * MAXP, HD)
    return pl.pallas_call(
        pick_kernel,
        out_shape=jax.ShapeDtypeStruct(shape, jnp.bfloat16),
        in_specs=[VMEM, VMEM, ANY],
        out_specs=HBM,
        scratch_shapes=[
            pltpu.VMEM((held.shape[0] * 2 * ROWS, HD), jnp.float32),
            pltpu.VMEM(shape, jnp.bfloat16),
            pltpu.SemaphoreType.DMA((PICK_STEPS,)),
        ],
        compiler_params=PARAMS,
        name="pick_pages",
    )(chosen, held, seen)


HEADS_PER_STEP = 8
CHUNK_WIDE = 8


def contract_last(left, right):
    return lax.dot_general(
        left, right, (((1,), (1,)), ((), ())), preferred_element_type=jnp.float32
    )


def attend_kernel(
    query_ref, key_ref, value_ref, held_ref, seen_ref, out_hbm, keys_ref, values_ref, mixed_ref, sems
):
    tokens = key_ref.shape[0]
    group = query_ref.shape[1] // HD
    rows = HEADS_PER_STEP * tokens
    width = HEADS_PER_STEP * HD
    half = PIECE * MAXP
    count = CHUNK_WIDE * half
    chunks = WIDE // CHUNK_WIDE
    steps = group // HEADS_PER_STEP

    def leave(step):
        columns = pl.ds(step * width, width)
        return pltpu.make_async_copy(mixed_ref.at[step], out_hbm.at[:, columns], sems.at[step])

    first_key = held_ref[0, :MAXP][:1]
    for chunk in range(chunks):
        wide = slice(chunk * CHUNK_WIDE, (chunk + 1) * CHUNK_WIDE)
        at = slice(chunk * count, (chunk + 1) * count)
        seen = seen_ref[at]
        visible = seen > 0
        keys_ref[at] = jnp.where(visible, held_ref[wide, :half].reshape(count, HD), first_key)
        values = held_ref[wide, half:].reshape(count, HD)
        values_ref[at, :HD] = jnp.where(visible, values, jnp.zeros_like(values))
        values_ref[at, HD:] = seen
    fresh_values = jnp.concatenate(
        [value_ref[...], jnp.ones((tokens, HD), jnp.bfloat16)], axis=1
    )
    token = lax.broadcasted_iota(jnp.int32, (rows, tokens), 0) % tokens
    causal = lax.broadcasted_iota(jnp.int32, (rows, tokens), 1) <= token
    for step in range(steps):
        query = jnp.concatenate(
            [
                query_ref[:, head * HD : (head + 1) * HD]
                for head in range(step * HEADS_PER_STEP, (step + 1) * HEADS_PER_STEP)
            ],
            axis=0,
        )
        fresh = jnp.where(causal, contract_last(query, key_ref[...]), HIDDEN)
        scores = [
            contract_last(query, keys_ref[chunk * count : (chunk + 1) * count])
            for chunk in range(chunks)
        ]
        top = functools.reduce(jnp.maximum, scores)
        highest = jnp.maximum(
            jnp.max(top, axis=1, keepdims=True), jnp.max(fresh, axis=1, keepdims=True)
        )
        mixed = jnp.dot(
            jnp.exp2((fresh - highest) * EXP2_SCALE).astype(jnp.bfloat16),
            fresh_values,
            preferred_element_type=jnp.float32,
        )
        weights = [jnp.exp2((part - highest) * EXP2_SCALE).astype(jnp.bfloat16) for part in scores]
        mixed += jnp.dot(
            jnp.concatenate(weights, axis=1), values_ref[...], preferred_element_type=jnp.float32
        )
        mixed = (mixed[:, :HD] / mixed[:, HD:]).astype(jnp.bfloat16)
        for n in range(HEADS_PER_STEP):
            mixed_ref[step, :, n * HD : (n + 1) * HD] = mixed[n * tokens : (n + 1) * tokens]
        leave(step).start()
    for step in range(steps):
        leave(step).wait()


def attend(query, key_new, value_new, held, seen):
    tokens, width = query.shape
    keys = WIDE * PIECE * MAXP
    steps = width // HD // HEADS_PER_STEP
    return pl.pallas_call(
        attend_kernel,
        out_shape=jax.ShapeDtypeStruct((tokens, width), jnp.bfloat16),
        in_specs=[VMEM] * 5,
        out_specs=HBM,
        scratch_shapes=[
            pltpu.VMEM((keys, HD), jnp.bfloat16),
            pltpu.VMEM((keys, 2 * HD), jnp.bfloat16),
            pltpu.VMEM((steps, tokens, HEADS_PER_STEP * HD), jnp.bfloat16),
            pltpu.SemaphoreType.DMA((steps,)),
        ],
        compiler_params=PARAMS,
        name="attend",
    )(query, key_new, value_new, held, seen)


def exchange(array, axes):
    return lax.all_to_all(array, axes, split_axis=0, concat_axis=0, tiled=True)


def body(query, key_new, value_new, key_cache, value_cache, page_table, prefix_len):
    own_request = lax.axis_index(WIDE_AXES)
    length = jnp.take(prefix_len, own_request)
    at = jnp.arange(WIDE * PIECE * MAXP, dtype=jnp.int32)
    seen = at % MAXP * PAGE + at // MAXP < length
    seen = jnp.broadcast_to(seen[:, None], (at.shape[0], HD)).astype(jnp.bfloat16)
    sources = WIDE * HEADS
    pages = page_table.reshape(-1)
    column = pages % STORED * sources + pages // STORED
    every = jnp.arange(STORED * sources, dtype=jnp.int32)
    chosen = (column[:, None] == every[None, :]).astype(jnp.bfloat16)
    pieces = split_pages(key_cache, value_cache).reshape(sources, ROWS, HD)
    pieces = exchange(pieces, WIDE_AXES + HEAD_AXES)
    picked = pick_pages(chosen, pieces.reshape(sources // 2, 2 * ROWS, HD), seen)
    held = exchange(picked, WIDE_AXES)
    return attend(query, key_new, value_new, held, seen)


def solution(mesh):
    fine = Mesh(mesh.devices.reshape(Y_LO, X, Z, Y_HI, CORE), WIDE_AXES + HEAD_AXES)
    in_specs = (
        P(WIDE_AXES, HEAD_AXES),
        P(WIDE_AXES, HEAD_AXES),
        P(WIDE_AXES, HEAD_AXES),
        P(WIDE_AXES + HEAD_AXES, None, None),
        P(WIDE_AXES + HEAD_AXES, None, None),
        P(),
        P(),
    )
    return jax.shard_map(
        body,
        mesh=fine,
        in_specs=in_specs,
        out_specs=P(WIDE_AXES, HEAD_AXES),
        check_vma=False,
    )
```

```python
import functools
import math

import jax
import jax.numpy as jnp
from jax import lax
from jax.experimental import pallas as pl
from jax.experimental.pallas import tpu as pltpu
from jax.sharding import Mesh, PartitionSpec as P

Y_LO, X, Z = 2, 4, 8
Y_HI, CORE = 4, 2
WIDE_AXES, HEAD_AXES = ("y_lo", "x", "z"), ("y_hi", "core")
WIDE = Y_LO * X * Z
HEADS = Y_HI * CORE
HD = 128
PAGE = 128
MAXP = 16
STORED = 2
PIECE = PAGE // WIDE
ROWS = STORED * 2 * PIECE
HIDDEN = -1e30
EXP2_SCALE = math.log2(math.e) / math.sqrt(HD)
PARAMS = pltpu.CompilerParams(vmem_limit_bytes=40 * 2**20)
ALL_PARAMS = pltpu.CompilerParams(vmem_limit_bytes=63 * 2**20)
VMEM = pl.BlockSpec(memory_space=pltpu.VMEM)
HBM = pl.BlockSpec(memory_space=pltpu.HBM)
ANY = pl.BlockSpec(memory_space=pl.ANY)

PARTS = 2
PART_TOKENS = PAGE // PARTS
PART_WIDE = WIDE // PARTS


def split_kernel(key_hbm, value_hbm, out_hbm, cache, ready, in_sems, out_sems):
    def fetch(part, kind):
        tokens = pl.ds(part * PART_TOKENS, PART_TOKENS)
        source = (key_hbm, value_hbm)[kind]
        return pltpu.make_async_copy(
            source.at[:, tokens], cache.at[kind, :, tokens], in_sems.at[part, kind]
        )

    def leave(part):
        rows = pl.ds(part * PART_WIDE, PART_WIDE)
        return pltpu.make_async_copy(ready.at[rows], out_hbm.at[rows], out_sems.at[part])

    for part in range(PARTS):
        for kind in range(2):
            fetch(part, kind).start()
    count = PART_WIDE * ROWS
    at = lax.broadcasted_iota(jnp.int32, (count, count), 0)
    source_row = (at % ROWS // PIECE) * PART_TOKENS + at // ROWS * PIECE + at % PIECE
    moved = source_row == lax.broadcasted_iota(jnp.int32, (count, count), 1)
    moved = jnp.where(moved, 1.0, 0.0).astype(jnp.bfloat16)
    for part in range(PARTS):
        for kind in range(2):
            fetch(part, kind).wait()
        tokens = slice(part * PART_TOKENS, (part + 1) * PART_TOKENS)
        rows = jnp.concatenate(
            [cache[kind, page, tokens] for page in range(STORED) for kind in range(2)], axis=0
        )
        rows = jnp.dot(moved, rows, preferred_element_type=jnp.float32)
        for pair in range(HEADS // 2):
            both = [
                rows[:, head * HD : (head + 1) * HD].reshape(PART_WIDE, ROWS, HD)
                for head in (2 * pair, 2 * pair + 1)
            ]
            ready[part * PART_WIDE : (part + 1) * PART_WIDE, pair] = jnp.concatenate(
                both, axis=1
            ).astype(jnp.bfloat16)
        leave(part).start()
    for part in range(PARTS):
        leave(part).wait()


def split_pages(key_cache, value_cache):
    shape = (WIDE, HEADS // 2, 2 * ROWS, HD)
    return pl.pallas_call(
        split_kernel,
        out_shape=jax.ShapeDtypeStruct(shape, jnp.bfloat16),
        in_specs=[HBM, HBM],
        out_specs=HBM,
        scratch_shapes=[
            pltpu.VMEM((2,) + key_cache.shape, jnp.bfloat16),
            pltpu.VMEM(shape, jnp.bfloat16),
            pltpu.SemaphoreType.DMA((PARTS, 2)),
            pltpu.SemaphoreType.DMA((PARTS,)),
        ],
        compiler_params=ALL_PARAMS,
        name="split_pages",
    )(key_cache, value_cache)


PICK_REQUESTS = 32
PICK_STEPS = WIDE // PICK_REQUESTS


def pick_kernel(chosen_ref, held_ref, seen_any, ready, spread):
    del seen_any
    sources = held_ref.shape[0] * 2
    spread[...] = held_ref[...].reshape(sources * ROWS, HD).astype(jnp.float32)
    columns = []
    for quarter in range(2 * PIECE):
        column = [
            spread[pl.ds(page * 2 * PIECE + quarter, sources, stride=ROWS), :]
            for page in range(STORED)
        ]
        columns.append(jnp.concatenate(column, axis=0).astype(jnp.bfloat16))
    columns = jnp.concatenate(columns, axis=1)
    for step in range(PICK_STEPS):
        first = step * PICK_REQUESTS
        picked = jnp.dot(
            chosen_ref[first * MAXP : (first + PICK_REQUESTS) * MAXP],
            columns,
            preferred_element_type=jnp.float32,
        ).astype(jnp.bfloat16)
        for request in range(PICK_REQUESTS):
            for quarter in range(2 * PIECE):
                ready[first + request, quarter * MAXP : (quarter + 1) * MAXP] = picked[
                    request * MAXP : (request + 1) * MAXP, quarter * HD : (quarter + 1) * HD
                ]


def pick_pages(chosen, held, seen):
    shape = (WIDE, 2 * PIECE * MAXP, HD)
    return pl.pallas_call(
        pick_kernel,
        out_shape=jax.ShapeDtypeStruct(shape, jnp.bfloat16),
        in_specs=[VMEM, VMEM, ANY],
        out_specs=VMEM,
        scratch_shapes=[
            pltpu.VMEM((held.shape[0] * 2 * ROWS, HD), jnp.float32),
        ],
        compiler_params=PARAMS,
        name="pick_pages",
    )(chosen, held, seen)


HEADS_PER_STEP = 8
CHUNK_WIDE = 8


def contract_last(left, right):
    return lax.dot_general(
        left, right, (((1,), (1,)), ((), ())), preferred_element_type=jnp.float32
    )


def attend_kernel(
    query_ref, key_ref, value_ref, held_ref, seen_ref, out_hbm, keys_ref, values_ref, mixed_ref, sems
):
    tokens = key_ref.shape[0]
    group = query_ref.shape[1] // HD
    rows = HEADS_PER_STEP * tokens
    width = HEADS_PER_STEP * HD
    half = PIECE * MAXP
    count = CHUNK_WIDE * half
    chunks = WIDE // CHUNK_WIDE
    steps = group // HEADS_PER_STEP

    def leave(step):
        columns = pl.ds(step * width, width)
        return pltpu.make_async_copy(mixed_ref.at[step], out_hbm.at[:, columns], sems.at[step])

    first_key = held_ref[0, :MAXP][:1]
    for chunk in range(chunks):
        wide = slice(chunk * CHUNK_WIDE, (chunk + 1) * CHUNK_WIDE)
        at = slice(chunk * count, (chunk + 1) * count)
        seen = seen_ref[at]
        visible = seen > 0
        keys_ref[at] = jnp.where(visible, held_ref[wide, :half].reshape(count, HD), first_key)
        values = held_ref[wide, half:].reshape(count, HD)
        values_ref[at, :HD] = jnp.where(visible, values, jnp.zeros_like(values))
        values_ref[at, HD:] = seen
    fresh_values = jnp.concatenate(
        [value_ref[...], jnp.ones((tokens, HD), jnp.bfloat16)], axis=1
    )
    token = lax.broadcasted_iota(jnp.int32, (rows, tokens), 0) % tokens
    causal = lax.broadcasted_iota(jnp.int32, (rows, tokens), 1) <= token
    for step in range(steps):
        query = jnp.concatenate(
            [
                query_ref[:, head * HD : (head + 1) * HD]
                for head in range(step * HEADS_PER_STEP, (step + 1) * HEADS_PER_STEP)
            ],
            axis=0,
        )
        fresh = jnp.where(causal, contract_last(query, key_ref[...]), HIDDEN)
        scores = [
            contract_last(query, keys_ref[chunk * count : (chunk + 1) * count])
            for chunk in range(chunks)
        ]
        top = functools.reduce(jnp.maximum, scores)
        highest = jnp.maximum(
            jnp.max(top, axis=1, keepdims=True), jnp.max(fresh, axis=1, keepdims=True)
        )
        mixed = jnp.dot(
            jnp.exp2((fresh - highest) * EXP2_SCALE).astype(jnp.bfloat16),
            fresh_values,
            preferred_element_type=jnp.float32,
        )
        weights = [jnp.exp2((part - highest) * EXP2_SCALE).astype(jnp.bfloat16) for part in scores]
        mixed += jnp.dot(
            jnp.concatenate(weights, axis=1), values_ref[...], preferred_element_type=jnp.float32
        )
        mixed = (mixed[:, :HD] / mixed[:, HD:]).astype(jnp.bfloat16)
        for n in range(HEADS_PER_STEP):
            mixed_ref[step, :, n * HD : (n + 1) * HD] = mixed[n * tokens : (n + 1) * tokens]
        leave(step).start()
    for step in range(steps):
        leave(step).wait()


def attend(query, key_new, value_new, held, seen):
    tokens, width = query.shape
    keys = WIDE * PIECE * MAXP
    steps = width // HD // HEADS_PER_STEP
    return pl.pallas_call(
        attend_kernel,
        out_shape=jax.ShapeDtypeStruct((tokens, width), jnp.bfloat16),
        in_specs=[VMEM] * 5,
        out_specs=HBM,
        scratch_shapes=[
            pltpu.VMEM((keys, HD), jnp.bfloat16),
            pltpu.VMEM((keys, 2 * HD), jnp.bfloat16),
            pltpu.VMEM((steps, tokens, HEADS_PER_STEP * HD), jnp.bfloat16),
            pltpu.SemaphoreType.DMA((steps,)),
        ],
        compiler_params=PARAMS,
        name="attend",
    )(query, key_new, value_new, held, seen)


def exchange(array, axes):
    return lax.all_to_all(array, axes, split_axis=0, concat_axis=0, tiled=True)


def body(query, key_new, value_new, key_cache, value_cache, page_table, prefix_len):
    own_request = lax.axis_index(WIDE_AXES)
    length = jnp.take(prefix_len, own_request)
    at = jnp.arange(WIDE * PIECE * MAXP, dtype=jnp.int32)
    seen = at % MAXP * PAGE + at // MAXP < length
    seen = jnp.broadcast_to(seen[:, None], (at.shape[0], HD)).astype(jnp.bfloat16)
    sources = WIDE * HEADS
    pages = page_table.reshape(-1)
    column = pages % STORED * sources + pages // STORED
    every = jnp.arange(STORED * sources, dtype=jnp.int32)
    chosen = (column[:, None] == every[None, :]).astype(jnp.bfloat16)
    pieces = split_pages(key_cache, value_cache).reshape(sources, ROWS, HD)
    pieces = exchange(pieces, WIDE_AXES + HEAD_AXES)
    picked = pick_pages(chosen, pieces.reshape(sources // 2, 2 * ROWS, HD), seen)
    held = exchange(picked, WIDE_AXES)
    return attend(query, key_new, value_new, held, seen)


def solution(mesh):
    fine = Mesh(mesh.devices.reshape(Y_LO, X, Z, Y_HI, CORE), WIDE_AXES + HEAD_AXES)
    in_specs = (
        P(WIDE_AXES, HEAD_AXES),
        P(WIDE_AXES, HEAD_AXES),
        P(WIDE_AXES, HEAD_AXES),
        P(WIDE_AXES + HEAD_AXES, None, None),
        P(WIDE_AXES + HEAD_AXES, None, None),
        P(),
        P(),
    )
    return jax.shard_map(
        body,
        mesh=fine,
        in_specs=in_specs,
        out_specs=P(WIDE_AXES, HEAD_AXES),
        check_vma=False,
    )
```
